32 devices in a mesh: row: 2 (over x), col: 16 (over z, y, core).
Axes of the slice: x: 2, y: 2, z: 4, core: 2. Of those that a mesh axis runs over, the one named last changes fastest.
Arguments:
- matrix: float32 [16384, 16384], P('row', 'col'), may hold values from -6 to 6, as said below
- vectors: float32 [2, 16384, 128], P(None, ('row', 'col')), may hold values from -0.16 to 0.16
- tfactor: float32 [2, 128, 128], replicated, may hold values from -0.5 to 0.5
Outputs:
- updated: float32 [16384, 16384], P('row', 'col')
The draws below stay inside these ranges and needn't reach their ends.
Inputs may be any that keep to these rules, and one draw needn't show every extreme that they name: matrix is symmetric: matrix[i, j] equals matrix[j, i].
All inputs are finite; a program needn't handle non-finite values.
Results may differ from the reference program's by a relative error of at most 0.00012.
Values sent between devices are 32-bit elements; how exact they have to be, the bound alone decides.
No kernel may reach another device: no remote copies, remote signals or barrier semaphores. Data moves between devices by JAX's collectives and lax.ppermute only.
A program may use at most 192 MiB of HBM per device.

```python
import jax
import jax.numpy as jnp
from jax import lax

NA = 16384
B = 128
PANELS = 2


def draw_matrix(key, part):
    first = jax.random.fold_in(key, 7101)
    noise = jax.random.normal(first, (NA, NA), jnp.float32)
    sym = (noise + noise.T) * 0.7071
    sym = jnp.clip(sym, -6.0, 6.0)
    sym = sym.at[0, NA - 1].set(6.0).at[NA - 1, 0].set(6.0)
    sym = sym.at[1, 2].set(-6.0).at[2, 1].set(-6.0)
    return sym.astype(jnp.float32)


def block_levels(own_key, dims, pieces, low, top_value):
    def one(dim, shards_of):
        heights = jax.random.uniform(jax.random.fold_in(jax.random.fold_in(own_key, 6), dim), (shards_of,), jnp.float32, low / len(pieces), top_value / len(pieces))
        return jnp.repeat(jnp.exp(heights), dims[dim] // shards_of).reshape((-1,) + (1,) * (len(dims) - dim - 1))

    loudness = one(*pieces[0])
    for cut in pieces[1:]:
        loudness = loudness * one(*cut)
    return loudness


def normal_values(key, shape, spread, most, pieces=(), kind=jnp.bfloat16):
    gain = block_levels(key, shape, pieces, -0.22, 0.18) if pieces else 1.0
    drawn = jax.random.normal(key, shape, jnp.float32) * spread * gain
    return jnp.minimum(jnp.maximum(drawn, -most), most).astype(kind)


def setup_inputs(seed: int = 0) -> dict:
    key_list = jax.random.split(jax.random.key(seed), 4)
    matrix = draw_matrix(jax.random.fold_in(key_list[3], 71), 0)
    vectors = normal_values(key_list[1], (PANELS, NA, B), (0.026 + 0.1 * min(1, 16384 // NA // 64)), 0.16, ((1, 32),), jnp.float32)
    tfactor = normal_values(key_list[2], (PANELS, B, B), B ** -0.5, 0.5, (), jnp.float32)
    return {"matrix": matrix, "vectors": vectors, "tfactor": tfactor}


highest = lax.Precision.HIGHEST


def mat_product(left, right):
    return jnp.dot(left, right, precision=highest, preferred_element_type=jnp.float32)


def reference(matrix, vectors, tfactor):
    current = matrix
    for panel_index in range(PANELS):
        vector = vectors[panel_index]
        factor = jnp.triu(tfactor[panel_index])
        product = mat_product(current, vector)
        ymatrix = mat_product(product, factor)
        gram_matrix = mat_product(vector.T, ymatrix)
        wmatrix = ymatrix - 0.5 * mat_product(vector, mat_product(factor.T, gram_matrix))
        blocks = current.reshape(8, NA // 8, NA)
        v_blocks = vector.reshape(8, NA // 8, B)
        w_blocks = wmatrix.reshape(8, NA // 8, B)

        def update(members, vector=vector, wmatrix=wmatrix):
            row_block, v_rows, w_rows = members
            return row_block - mat_product(v_rows, wmatrix.T) - mat_product(w_rows, vector.T)

        current = lax.map(update, (blocks, v_blocks, w_blocks)).reshape(NA, NA)
    return current
```

```python
import functools

import jax
import jax.numpy as jnp
from jax import lax
from jax.experimental import pallas as pl
from jax.experimental.pallas import tpu as pltpu
from jax.sharding import PartitionSpec as P

highest = lax.Precision.HIGHEST
f32 = jnp.float32
bf16 = jnp.bfloat16
VMEM_LIMIT = 48 * 1024 * 1024


def split(value):
    high = value.astype(bf16)
    low = (value - high.astype(f32)).astype(bf16)
    return high, low


def dot(left, right):
    return jnp.dot(left, right, preferred_element_type=f32)


def exact(left, right):
    return jnp.dot(left, right, precision=highest, preferred_element_type=f32)


def exact_nt(left, right):
    return lax.dot_general(left, right, (((1,), (1,)), ((), ())), precision=highest, preferred_element_type=f32)


def row_block(rows):
    return min(rows, 512)


def product_kernel(a_ref, v_ref, out_ref):
    @pl.when(pl.program_id(0) == 0)
    def _():
        out_ref[...] = jnp.zeros_like(out_ref)

    v = jnp.concatenate([v_ref[p] for p in range(v_ref.shape[0])], axis=1)
    v_hi, v_lo = split(v.T)
    a_hi, a_lo = split(a_ref[...])
    wide = v_hi.shape[0]
    both = dot(jnp.concatenate([v_hi, v_lo], axis=0), a_hi)
    out_ref[...] += both[:wide] + (both[wide:] + dot(v_hi, a_lo))


def product(a, v):
    rows, cols = a.shape
    panels, _, b = v.shape
    block = row_block(rows)
    return pl.pallas_call(
        product_kernel,
        grid=(rows // block,),
        in_specs=[
            pl.BlockSpec((block, cols), lambda i: (i, 0)),
            pl.BlockSpec((panels, block, b), lambda i: (0, i, 0)),
        ],
        out_specs=pl.BlockSpec((panels * b, cols), lambda i: (0, 0)),
        out_shape=jax.ShapeDtypeStruct((panels * b, cols), f32),
        compiler_params=pltpu.CompilerParams(vmem_limit_bytes=VMEM_LIMIT),
        name="product",
    )(a, v)


def sum_rows(mine, other):
    wide, cols = mine.shape

    def kernel(mine_ref, other_ref, sum_ref, z_ref):
        total = mine_ref[...] + other_ref[...]
        sum_ref[...] = total
        z_ref[...] = total.T

    return pl.pallas_call(
        kernel,
        out_shape=(jax.ShapeDtypeStruct((wide, cols), f32), jax.ShapeDtypeStruct((cols, wide), f32)),
        compiler_params=pltpu.CompilerParams(vmem_limit_bytes=VMEM_LIMIT),
        name="sum_rows",
    )(mine, other)


def gram_kernel(v_ref, z_ref, out_ref, cross_ref):
    @pl.when(pl.program_id(0) == 0)
    def _():
        out_ref[...] = jnp.zeros_like(out_ref)
        cross_ref[...] = jnp.zeros_like(cross_ref)

    v = jnp.concatenate([v_ref[p] for p in range(v_ref.shape[0])], axis=1)
    vt_hi, vt_lo = split(v.T)
    v_hi, v_lo = split(v)
    z_hi, z_lo = split(z_ref[...])
    b = v_ref.shape[2]
    out_ref[...] += dot(vt_hi, z_hi) + (dot(vt_lo, z_hi) + dot(vt_hi, z_lo))
    cross_ref[...] += dot(vt_hi[:b], v_hi[:, b:]) + (dot(vt_lo[:b], v_hi[:, b:]) + dot(vt_hi[:b], v_lo[:, b:]))


def gram(v, z):
    panels, rows, b = v.shape
    wide = panels * b
    block = row_block(rows)
    return pl.pallas_call(
        gram_kernel,
        grid=(rows // block,),
        in_specs=[
            pl.BlockSpec((panels, block, b), lambda i: (0, i, 0)),
            pl.BlockSpec((block, wide), lambda i: (i, 0)),
        ],
        out_specs=[
            pl.BlockSpec((wide, wide), lambda i: (0, 0)),
            pl.BlockSpec((b, b), lambda i: (0, 0)),
        ],
        out_shape=(jax.ShapeDtypeStruct((wide, wide), f32), jax.ShapeDtypeStruct((b, b), f32)),
        compiler_params=pltpu.CompilerParams(vmem_limit_bytes=VMEM_LIMIT),
        name="gram",
    )(v, z)


def factor_kernel(t_ref, m_ref, n_ref, zt_ref, vc_ref, hi_ref, lo_ref):
    b = t_ref.shape[1]
    upper = lax.broadcasted_iota(jnp.int32, (b, b), 0) <= lax.broadcasted_iota(jnp.int32, (b, b), 1)
    t1 = jnp.where(upper, t_ref[0], 0.0)
    t2 = jnp.where(upper, t_ref[1], 0.0)
    n = n_ref[...]
    m11, m12, m22 = m_ref[:b, :b], m_ref[:b, b:], m_ref[b:, b:]
    k1 = exact(t1.T, exact(m11, t1))
    e = exact(t1.T, m12) - 0.5 * exact(k1.T, n)
    nte = exact(n.T, e)
    k2 = exact(t2.T, exact(m22 - nte - nte.T, t2))
    s12 = -exact(t1, exact(n, t2))
    r11 = -0.5 * k1
    r12 = exact(0.5 * exact(k1, n) - e, t2)
    r22 = -0.5 * k2
    s = jnp.concatenate([jnp.concatenate([t1, s12], 1), jnp.concatenate([jnp.zeros_like(t1), t2], 1)], 0)
    r = jnp.concatenate([jnp.concatenate([r11 + r11.T, r12], 1), jnp.concatenate([r12.T, r22 + r22.T], 1)], 0)
    vct = jnp.concatenate([vc_ref[0], vc_ref[1]], axis=1).T
    pt = exact(s.T, zt_ref[...]) + exact(r, vct)
    qt = exact(s, vct)
    wide = 2 * b
    hi_ref[:wide], lo_ref[:wide] = split(pt)
    hi_ref[wide:], lo_ref[wide:] = split(qt)


def factors(tfactor, m, n, zt, vc):
    wide, cols = zt.shape
    out = jax.ShapeDtypeStruct((2 * wide, cols), bf16)
    return pl.pallas_call(
        factor_kernel,
        out_shape=(out, out),
        compiler_params=pltpu.CompilerParams(vmem_limit_bytes=VMEM_LIMIT),
        name="factors",
    )(tfactor, m, n, zt, vc)


def update_kernel(a_ref, v_ref, z_ref, hi_ref, lo_ref, out_ref):
    left = jnp.concatenate([v_ref[p] for p in range(v_ref.shape[0])] + [z_ref[...]], axis=1)
    l_hi, l_lo = split(left)
    hi = hi_ref[...]
    out_ref[...] = a_ref[...] - (dot(l_hi, hi) + (dot(l_lo, hi) + dot(l_hi, lo_ref[...])))


def update(a, v, z, hi, lo):
    rows, cols = a.shape
    panels, _, b = v.shape
    block = row_block(rows)
    wide = panels * b
    return pl.pallas_call(
        update_kernel,
        grid=(rows // block,),
        in_specs=[
            pl.BlockSpec((block, cols), lambda i: (i, 0)),
            pl.BlockSpec((panels, block, b), lambda i: (0, i, 0)),
            pl.BlockSpec((block, wide), lambda i: (i, 0)),
            pl.BlockSpec((2 * wide, cols), lambda i: (0, 0)),
            pl.BlockSpec((2 * wide, cols), lambda i: (0, 0)),
        ],
        out_specs=pl.BlockSpec((block, cols), lambda i: (i, 0)),
        out_shape=jax.ShapeDtypeStruct((rows, cols), f32),
        compiler_params=pltpu.CompilerParams(vmem_limit_bytes=VMEM_LIMIT),
        name="update",
    )(a, v, z, hi, lo)


def row_sum(value):
    total = lax.axis_size("row")
    if total == 2:
        return lax.ppermute(value, "row", [(0, 1), (1, 0)])
    return lax.psum(value, "row") - value


def body(matrix, vectors, tfactor):
    rows_here, cols_here = matrix.shape
    own = vectors.shape[1]
    row_total, col_total = lax.axis_size("row"), lax.axis_size("col")
    row, col = lax.axis_index("row"), lax.axis_index("col")
    owner = col * row_total // col_total
    offset = col * cols_here - owner * rows_here

    v_rows = lax.all_gather(vectors, "col", axis=1, tiled=True)
    mine = lax.dynamic_slice_in_dim(v_rows, offset, cols_here, 1)
    v_cols = mine
    for shift in range(1, row_total):
        other = lax.ppermute(mine, "row", [(i, (i + shift) % row_total) for i in range(row_total)])
        v_cols = jnp.where((row - owner) % row_total == shift, other, v_cols)

    part = product(matrix, v_rows)
    zt, z = sum_rows(part, row_sum(part))

    per_row = col_total // row_total
    z_own = None
    for piece in range(row_total):
        pairs = []
        for r in range(row_total):
            for c in range(per_row):
                pairs.append((r * col_total + r * per_row + c, r * col_total + c * row_total + piece))
        sent = lax.ppermute(z[piece * own : (piece + 1) * own], ("row", "col"), pairs)
        z_own = sent if z_own is None else z_own + sent
    z_rows = lax.all_gather(z_own, "col", axis=0, tiled=True)

    m, n = gram(v_rows, z_rows)
    small = jnp.concatenate([m, jnp.concatenate([n, jnp.zeros_like(n)], 1)], 0)
    small = small + row_sum(small)
    b = n.shape[0]
    hi, lo = factors(tfactor, small[: 2 * b], small[2 * b :, :b], zt, v_cols)
    return update(matrix, v_rows, z_rows, hi, lo)


def solution(mesh):
    return jax.shard_map(
        body,
        mesh=mesh,
        in_specs=(P("row", "col"), P(None, ("row", "col"), None), P()),
        out_specs=P("row", "col"),
        check_vma=False,
    )
```

```python
import functools

import jax
import jax.numpy as jnp
from jax import lax
from jax.experimental import pallas as pl
from jax.experimental.pallas import tpu as pltpu
from jax.sharding import PartitionSpec as P

highest = lax.Precision.HIGHEST
f32 = jnp.float32
bf16 = jnp.bfloat16
VMEM_LIMIT = 48 * 1024 * 1024


def split(value):
    high = value.astype(bf16)
    low = (value - high.astype(f32)).astype(bf16)
    return high, low


def dot(left, right):
    return jnp.dot(left, right, preferred_element_type=f32)


def exact(left, right):
    return jnp.dot(left, right, precision=highest, preferred_element_type=f32)


def exact_nt(left, right):
    return lax.dot_general(left, right, (((1,), (1,)), ((), ())), precision=highest, preferred_element_type=f32)


def row_block(rows):
    return min(rows, 512)


def product_kernel(a_ref, v_ref, out_ref):
    @pl.when(pl.program_id(0) == 0)
    def _():
        out_ref[...] = jnp.zeros_like(out_ref)

    v = jnp.concatenate([v_ref[p] for p in range(v_ref.shape[0])], axis=1)
    v_hi, v_lo = split(v.T)
    a_hi, a_lo = split(a_ref[...])
    wide = v_hi.shape[0]
    both = dot(jnp.concatenate([v_hi, v_lo], axis=0), a_hi)
    out_ref[...] += both[:wide] + (both[wide:] + dot(v_hi, a_lo))


def product(a, v):
    rows, cols = a.shape
    panels, _, b = v.shape
    block = row_block(rows)
    return pl.pallas_call(
        product_kernel,
        grid=(rows // block,),
        in_specs=[
            pl.BlockSpec((block, cols), lambda i: (i, 0)),
            pl.BlockSpec((panels, block, b), lambda i: (0, i, 0)),
        ],
        out_specs=pl.BlockSpec((panels * b, cols), lambda i: (0, 0)),
        out_shape=jax.ShapeDtypeStruct((panels * b, cols), f32),
        compiler_params=pltpu.CompilerParams(vmem_limit_bytes=VMEM_LIMIT),
        name="product",
    )(a, v)


def sum_rows(mine, other):
    wide, cols = mine.shape

    def kernel(mine_ref, other_ref, sum_ref, z_ref):
        total = mine_ref[...] + other_ref[...]
        sum_ref[...] = total
        z_ref[...] = total.T

    return pl.pallas_call(
        kernel,
        out_shape=(jax.ShapeDtypeStruct((wide, cols), f32), jax.ShapeDtypeStruct((cols, wide), f32)),
        compiler_params=pltpu.CompilerParams(vmem_limit_bytes=VMEM_LIMIT),
        name="sum_rows",
    )(mine, other)


def gram_kernel(v_ref, z_ref, out_ref, cross_ref):
    @pl.when(pl.program_id(0) == 0)
    def _():
        out_ref[...] = jnp.zeros_like(out_ref)
        cross_ref[...] = jnp.zeros_like(cross_ref)

    v = jnp.concatenate([v_ref[p] for p in range(v_ref.shape[0])], axis=1)
    vt_hi, vt_lo = split(v.T)
    v_hi, v_lo = split(v)
    z_hi, z_lo = split(z_ref[...])
    b = v_ref.shape[2]
    out_ref[...] += dot(vt_hi, z_hi) + (dot(vt_lo, z_hi) + dot(vt_hi, z_lo))
    cross_ref[...] += dot(vt_hi[:b], v_hi[:, b:]) + (dot(vt_lo[:b], v_hi[:, b:]) + dot(vt_hi[:b], v_lo[:, b:]))


def gram(v, z):
    panels, rows, b = v.shape
    wide = panels * b
    block = row_block(rows)
    return pl.pallas_call(
        gram_kernel,
        grid=(rows // block,),
        in_specs=[
            pl.BlockSpec((panels, block, b), lambda i: (0, i, 0)),
            pl.BlockSpec((block, wide), lambda i: (i, 0)),
        ],
        out_specs=[
            pl.BlockSpec((wide, wide), lambda i: (0, 0)),
            pl.BlockSpec((b, b), lambda i: (0, 0)),
        ],
        out_shape=(jax.ShapeDtypeStruct((wide, wide), f32), jax.ShapeDtypeStruct((b, b), f32)),
        compiler_params=pltpu.CompilerParams(vmem_limit_bytes=VMEM_LIMIT),
        name="gram",
    )(v, z)


def factor_kernel(t_ref, m_ref, n_ref, zt_ref, vc_ref, hi_ref, lo_ref):
    b = t_ref.shape[1]
    upper = lax.broadcasted_iota(jnp.int32, (b, b), 0) <= lax.broadcasted_iota(jnp.int32, (b, b), 1)
    t1 = jnp.where(upper, t_ref[0], 0.0)
    t2 = jnp.where(upper, t_ref[1], 0.0)
    n = n_ref[...]
    m11, m12, m22 = m_ref[:b, :b], m_ref[:b, b:], m_ref[b:, b:]
    k1 = exact(t1.T, exact(m11, t1))
    e = exact(t1.T, m12) - 0.5 * exact(k1.T, n)
    nte = exact(n.T, e)
    k2 = exact(t2.T, exact(m22 - nte - nte.T, t2))
    s12 = -exact(t1, exact(n, t2))
    r11 = -0.5 * k1
    r12 = exact(0.5 * exact(k1, n) - e, t2)
    r22 = -0.5 * k2
    s = jnp.concatenate([jnp.concatenate([t1, s12], 1), jnp.concatenate([jnp.zeros_like(t1), t2], 1)], 0)
    r = jnp.concatenate([jnp.concatenate([r11 + r11.T, r12], 1), jnp.concatenate([r12.T, r22 + r22.T], 1)], 0)
    vct = jnp.concatenate([vc_ref[0], vc_ref[1]], axis=1).T
    pt = exact(s.T, zt_ref[...]) + exact(r, vct)
    qt = exact(s, vct)
    wide = 2 * b
    hi_ref[:wide], lo_ref[:wide] = split(pt)
    hi_ref[wide:], lo_ref[wide:] = split(qt)


def factors(tfactor, m, n, zt, vc):
    wide, cols = zt.shape
    out = jax.ShapeDtypeStruct((2 * wide, cols), bf16)
    return pl.pallas_call(
        factor_kernel,
        out_shape=(out, out),
        compiler_params=pltpu.CompilerParams(vmem_limit_bytes=VMEM_LIMIT),
        name="factors",
    )(tfactor, m, n, zt, vc)


def update_kernel(a_ref, v_ref, z_ref, hi_ref, lo_ref, out_ref):
    left = jnp.concatenate([v_ref[p] for p in range(v_ref.shape[0])] + [z_ref[...]], axis=1)
    l_hi, l_lo = split(left)
    hi = hi_ref[...]
    out_ref[...] = a_ref[...] - (dot(l_hi, hi) + (dot(l_lo, hi) + dot(l_hi, lo_ref[...])))


def update(a, v, z, hi, lo):
    rows, cols = a.shape
    panels, _, b = v.shape
    block = row_block(rows)
    wide = panels * b
    return pl.pallas_call(
        update_kernel,
        grid=(rows // block,),
        in_specs=[
            pl.BlockSpec((block, cols), lambda i: (i, 0)),
            pl.BlockSpec((panels, block, b), lambda i: (0, i, 0)),
            pl.BlockSpec((block, wide), lambda i: (i, 0)),
            pl.BlockSpec((2 * wide, cols), lambda i: (0, 0)),
            pl.BlockSpec((2 * wide, cols), lambda i: (0, 0)),
        ],
        out_specs=pl.BlockSpec((block, cols), lambda i: (i, 0)),
        out_shape=jax.ShapeDtypeStruct((rows, cols), f32),
        compiler_params=pltpu.CompilerParams(vmem_limit_bytes=VMEM_LIMIT),
        name="update",
    )(a, v, z, hi, lo)


def row_sum(value):
    total = lax.axis_size("row")
    if total == 2:
        return lax.ppermute(value, "row", [(0, 1), (1, 0)])
    return lax.psum(value, "row") - value


def general_body(matrix, vectors, tfactor):
    rows_here, cols_here = matrix.shape
    own = vectors.shape[1]
    row_total, col_total = lax.axis_size("row"), lax.axis_size("col")
    row, col = lax.axis_index("row"), lax.axis_index("col")
    owner = col * row_total // col_total
    offset = col * cols_here - owner * rows_here

    v_rows = lax.all_gather(vectors, "col", axis=1, tiled=True)
    mine = lax.dynamic_slice_in_dim(v_rows, offset, cols_here, 1)
    v_cols = mine
    for shift in range(1, row_total):
        other = lax.ppermute(mine, "row", [(i, (i + shift) % row_total) for i in range(row_total)])
        v_cols = jnp.where((row - owner) % row_total == shift, other, v_cols)

    part = product(matrix, v_rows)
    zt, z = sum_rows(part, row_sum(part))

    per_row = col_total // row_total
    z_own = None
    for piece in range(row_total):
        pairs = []
        for r in range(row_total):
            for c in range(per_row):
                pairs.append((r * col_total + r * per_row + c, r * col_total + c * row_total + piece))
        sent = lax.ppermute(z[piece * own : (piece + 1) * own], ("row", "col"), pairs)
        z_own = sent if z_own is None else z_own + sent
    z_rows = lax.all_gather(z_own, "col", axis=0, tiled=True)

    m, n = gram(v_rows, z_rows)
    small = jnp.concatenate([m, jnp.concatenate([n, jnp.zeros_like(n)], 1)], 0)
    small = small + row_sum(small)
    b = n.shape[0]
    hi, lo = factors(tfactor, small[: 2 * b], small[2 * b :, :b], zt, v_cols)
    return update(matrix, v_rows, z_rows, hi, lo)


def ring_chip(position, chips):
    position %= chips
    return 2 * position if position < chips // 2 else 2 * (chips - 1 - position) + 1


def ring_chips_here(chips, steps):
    chip = lax.axis_index("col") // 2
    place = jnp.where(chip % 2 == 0, chip // 2, chips - 1 - chip // 2)

    def at(position):
        position = position % chips
        return jnp.where(position < chips // 2, 2 * position, 2 * (chips - 1 - position) + 1)

    core = lax.axis_index("col") % 2
    signs = 2 * core - 1
    return [at(place + signs * step) for step in steps], [at(place - signs * step) for step in steps]


def ring_gather(streams):
    chips = lax.axis_size("col") // 2
    core = lax.axis_index("col") % 2
    swap = [(c, c ^ 1) for c in range(2 * chips)]
    around = []
    for i in range(chips):
        around.append((2 * ring_chip(i, chips), 2 * ring_chip(i + 1, chips)))
        around.append((2 * ring_chip(i, chips) + 1, 2 * ring_chip(i - 1, chips) + 1))

    def joined(mine):
        other = lax.ppermute(mine, "col", swap)
        first, second = jnp.where(core == 0, mine, other), jnp.where(core == 0, other, mine)
        return jnp.concatenate([first, second], axis=0)

    held = [joined(mine) for mine in streams]
    result = [[block] for block in held]
    for _ in range(1, chips // 2):
        held = [lax.ppermute(block, "col", around) for block in held]
        for blocks, block in zip(result, held):
            blocks += [block, lax.ppermute(block, "col", swap)]
    for blocks, block in zip(result, held):
        rows = block.shape[0] // 2
        part = lax.dynamic_slice_in_dim(block, core * rows, rows, 0)
        blocks.append(joined(lax.ppermute(part, "col", around)))
    return result


def ring_order(chips):
    came, other = ring_chips_here(chips, range(chips // 2 + 1))
    order = [came[0]]
    for step in range(1, chips // 2):
        order += [came[step], other[step]]
    return order + [came[chips // 2]]


def part_kernel(count, first, index_ref, a_ref, *refs):
    values, refs = refs[: 2 * count], refs[2 * count :]
    if first:
        out_ref, v_ref = refs
    else:
        total_ref, _, out_ref, v_ref = refs
    step = pl.program_id(0)

    @pl.when(step == 0)
    def _():
        out_ref[...] = jnp.zeros_like(out_ref) if first else total_ref[...]

    for j in range(count):

        @pl.when(step == j)
        def _(j=j):
            v_ref[...] = jnp.concatenate([values[2 * j][...], values[2 * j + 1][...]], axis=1)

    v_hi, v_lo = split(v_ref[...].T)
    a_hi, a_lo = split(a_ref[...])
    wide = v_hi.shape[0]
    both = dot(jnp.concatenate([v_hi, v_lo], axis=0), a_hi)
    out_ref[...] += both[:wide] + (both[wide:] + dot(v_hi, a_lo))


def part_product(a, blocks, index, state):
    rows, cols = a.shape
    block, b = blocks[0][0].shape
    count = len(blocks)
    first = state is None
    wide = 2 * b
    whole = pl.BlockSpec((block, b), lambda i, index: (0, 0))
    total = pl.BlockSpec((wide, cols), lambda i, index: (0, 0))
    in_specs = [pl.BlockSpec((block, cols), lambda i, index: (index[i], 0))] + [whole] * (2 * count)
    operands = [value for pair in blocks for value in pair]
    aliases = {}
    if not first:
        in_specs += [total, pl.BlockSpec(memory_space=pl.ANY)]
        operands += list(state)
        aliases = {2 + 2 * count: 0, 3 + 2 * count: 1}
    return pl.pallas_call(
        functools.partial(part_kernel, count, first),
        grid_spec=pltpu.PrefetchScalarGridSpec(
            num_scalar_prefetch=1,
            grid=(count,),
            in_specs=in_specs,
            out_specs=[total, pl.BlockSpec((block, wide), lambda i, index: (index[i], 0))],
        ),
        out_shape=(jax.ShapeDtypeStruct((wide, cols), f32), jax.ShapeDtypeStruct((rows, wide), f32)),
        input_output_aliases=aliases,
        compiler_params=pltpu.CompilerParams(vmem_limit_bytes=VMEM_LIMIT),
        name="part_product",
    )(index, a, *operands)


def own_gram_kernel(index_ref, v_ref, z1_ref, z2_ref, out_ref):
    b = z1_ref.shape[1]
    v = v_ref[...]
    vt = v.T
    z = jnp.concatenate([z1_ref[...], z2_ref[...]], axis=1)
    out_ref[:b] = exact(vt[:b], z)
    out_ref[b:, :b] = exact(vt[:b], v[:, b:])
    out_ref[b:, b:] = exact(vt[b:], z[:, b:])


def own_gram(index, v, z1, z2):
    rows, b = z1.shape
    return pl.pallas_call(
        own_gram_kernel,
        grid_spec=pltpu.PrefetchScalarGridSpec(
            num_scalar_prefetch=1,
            grid=(1,),
            in_specs=[
                pl.BlockSpec((rows, 2 * b), lambda i, index: (index[0], 0)),
                pl.BlockSpec((rows, b), lambda i, index: (0, 0)),
                pl.BlockSpec((rows, b), lambda i, index: (0, 0)),
            ],
            out_specs=pl.BlockSpec((2 * b, 2 * b), lambda i, index: (0, 0)),
        ),
        out_shape=jax.ShapeDtypeStruct((2 * b, 2 * b), f32),
        compiler_params=pltpu.CompilerParams(vmem_limit_bytes=VMEM_LIMIT),
        name="own_gram",
    )(index, v, z1, z2)


def part_update_kernel(count, first, index_ref, a_ref, v_ref, hi_ref, lo_ref, *refs):
    values, out_ref = refs[: 2 * count], refs[-1]
    step = pl.program_id(0)
    rows = a_ref.shape[0]
    hi, lo = hi_ref[...], lo_ref[...]
    for j in range(2 * count):

        @pl.when(step == j)
        def _(j=j):
            here = pl.ds((j % 2) * rows, rows)
            left = jnp.concatenate([v_ref[...], values[j // 2 * 2][here, :], values[j // 2 * 2 + 1][here, :]], axis=1)
            l_hi, l_lo = split(left)
            out_ref[...] = a_ref[...] - (dot(l_hi, hi) + (dot(l_lo, hi) + dot(l_hi, lo)))


def part_update(a, v, hi, lo, blocks, index, state):
    rows, cols = a.shape
    wide = v.shape[1]
    count = len(blocks)
    span, b = blocks[0][0].shape
    block = span // 2
    first = state is None
    placed = lambda i, index: (index[i], 0)
    fixed = lambda i, index: (0, 0)
    in_specs = [
        pl.BlockSpec((block, cols), placed),
        pl.BlockSpec((block, wide), placed),
        pl.BlockSpec((2 * wide, cols), fixed),
        pl.BlockSpec((2 * wide, cols), fixed),
    ] + [pl.BlockSpec((span, b), fixed)] * (2 * count)
    operands = [a, v, hi, lo] + [value for pair in blocks for value in pair]
    aliases = {}
    if not first:
        in_specs.append(pl.BlockSpec(memory_space=pl.ANY))
        operands.append(state)
        aliases = {len(operands): 0}
    return pl.pallas_call(
        functools.partial(part_update_kernel, count, first),
        grid_spec=pltpu.PrefetchScalarGridSpec(
            num_scalar_prefetch=1,
            grid=(2 * count,),
            in_specs=in_specs,
            out_specs=pl.BlockSpec((block, cols), placed),
        ),
        out_shape=jax.ShapeDtypeStruct((rows, cols), f32),
        input_output_aliases=aliases,
        compiler_params=pltpu.CompilerParams(vmem_limit_bytes=VMEM_LIMIT),
        name="part_update",
    )(index, *operands)


def all_sum(value):
    cols = lax.axis_size("col")
    core = lax.axis_index("col") % 2
    swap = [(c, c ^ 1) for c in range(cols)]
    rows = value.shape[0] // 2
    keep = lax.dynamic_slice_in_dim(value, core * rows, rows, 0)
    give = lax.dynamic_slice_in_dim(value, (1 - core) * rows, rows, 0)
    keep = keep + lax.ppermute(give, "col", swap)
    keep = keep + lax.ppermute(keep, "row", [(0, 1), (1, 0)])
    bit = 2
    while bit < cols:
        keep = keep + lax.ppermute(keep, "col", [(c, c ^ bit) for c in range(cols)])
        bit *= 2
    other = lax.ppermute(keep, "col", swap)
    return jnp.concatenate([jnp.where(core == 0, keep, other), jnp.where(core == 0, other, keep)], axis=0)


def body(matrix, vectors, tfactor):
    rows_here, cols_here = matrix.shape
    own, b = vectors.shape[1:]
    cols = lax.axis_size("col")
    row, col = lax.axis_index("row"), lax.axis_index("col")
    chips = cols // 2
    half = chips // 2
    chip, core = col // 2, col % 2
    both = ("row", "col")

    order = ring_order(chips)
    v_blocks = list(zip(*ring_gather([vectors[0], vectors[1]])))
    state = None
    for begin, end in ((0, 3), (3, chips - 1), (chips - 1, chips)):
        state = part_product(matrix, v_blocks[begin:end], jnp.stack(order[begin:end]).astype(jnp.int32), state)
    part, v_rows = state

    keep = lax.dynamic_slice_in_dim(part, row * own, own, 1)
    give = lax.dynamic_slice_in_dim(part, (1 - row) * own, own, 1)
    across = [(0, 1), (1, 0)]
    sums = [keep[p * b : (p + 1) * b] + lax.ppermute(give[p * b : (p + 1) * b], "row", across) for p in range(2)]
    halves = [s.T for s in sums]

    def at(r, j, k):
        return r * cols + 2 * (j % chips) + k

    foreign = [(r, j, k) for r in range(2) for j in range((1 - r) * half, (2 - r) * half) for k in range(2)]
    direct = [(at(r, j, k), at(1 - r, j + half, k)) for r, j, k in foreign]
    along = [(at(r, j, k), at(r, j + half, k)) for r, j, k in foreign]
    over = [(at(r, j + half, k), at(1 - r, j + half, k)) for r, j, k in foreign]
    got1 = lax.ppermute(halves[0], both, direct)
    got2 = lax.ppermute(lax.ppermute(halves[1], both, along), both, over)
    home = chip // half == row
    z1 = jnp.where(home, halves[0], got1)
    z2 = jnp.where(home, halves[1], got2)

    def z_index(j, k):
        return 2 * (2 * (j % half) + k) + j // half

    small = all_sum(own_gram(z_index(chip, core).reshape(1).astype(jnp.int32), v_rows, z1, z2))

    owner = col // chips
    mine = lax.dynamic_slice_in_dim(v_rows, (col - owner * chips) * cols_here, cols_here, 0)
    mine, _ = lax.optimization_barrier((mine, z1))
    tile_pairs = [(r * cols + c, (1 - r) * cols + c) for r in range(2) for c in range(r * chips, (r + 1) * chips)]
    v_cols = jnp.where(owner == row, mine, lax.ppermute(mine, both, tile_pairs))
    sums = jnp.concatenate(sums, axis=0)
    others = lax.ppermute(sums, "row", across)
    zt = jnp.concatenate([jnp.where(row == 0, sums, others), jnp.where(row == 0, others, sums)], axis=1)

    z_blocks = list(zip(*ring_gather([z1, z2])))
    v_pair = jnp.stack([v_cols[:, :b], v_cols[:, b:]])
    hi, lo = factors(tfactor, small, small[b:, :b], zt, v_pair)
    out = None
    for begin, end in ((0, chips - 3), (chips - 3, chips - 1), (chips - 1, chips)):
        index = jnp.stack([z_index(j, k) for j in order[begin:end] for k in range(2)]).astype(jnp.int32)
        out = part_update(matrix, v_rows, hi, lo, z_blocks[begin:end], index, out)
    return out


def solution(mesh):
    rows, cols = mesh.shape["row"], mesh.shape["col"]
    pairs = rows == 2 and cols >= 8 and cols & (cols - 1) == 0
    return jax.shard_map(
        body if pairs else general_body,
        mesh=mesh,
        in_specs=(P("row", "col"), P(None, ("row", "col"), None), P()),
        out_specs=P("row", "col"),
        check_vma=False,
    )
```

```python
import functools

import jax
import jax.numpy as jnp
from jax import lax
from jax.experimental import pallas as pl
from jax.experimental.pallas import tpu as pltpu
from jax.sharding import PartitionSpec as P

highest = lax.Precision.HIGHEST
f32 = jnp.float32
bf16 = jnp.bfloat16
VMEM_LIMIT = 48 * 1024 * 1024


def split(value):
    high = value.astype(bf16)
    low = (value - high.astype(f32)).astype(bf16)
    return high, low


def dot(left, right):
    return jnp.dot(left, right, preferred_element_type=f32)


def exact(left, right):
    return jnp.dot(left, right, precision=highest, preferred_element_type=f32)


def exact_nt(left, right):
    return lax.dot_general(left, right, (((1,), (1,)), ((), ())), precision=highest, preferred_element_type=f32)


TOKEN = jax.ShapeDtypeStruct((8, 128), f32)
TOKEN_SPEC = pl.BlockSpec((8, 128), lambda i, index: (0, 0))


def cost(flops, count):
    return pl.CostEstimate(flops=flops, bytes_accessed=count, transcendentals=0)


def row_block(rows):
    return min(rows, 512)


def product_kernel(a_ref, v_ref, out_ref):
    @pl.when(pl.program_id(0) == 0)
    def _():
        out_ref[...] = jnp.zeros_like(out_ref)

    v = jnp.concatenate([v_ref[p] for p in range(v_ref.shape[0])], axis=1)
    v_hi, v_lo = split(v.T)
    a_hi, a_lo = split(a_ref[...])
    wide = v_hi.shape[0]
    both = dot(jnp.concatenate([v_hi, v_lo], axis=0), a_hi)
    out_ref[...] += both[:wide] + (both[wide:] + dot(v_hi, a_lo))


def product(a, v):
    rows, cols = a.shape
    panels, _, b = v.shape
    block = row_block(rows)
    return pl.pallas_call(
        product_kernel,
        grid=(rows // block,),
        in_specs=[
            pl.BlockSpec((block, cols), lambda i: (i, 0)),
            pl.BlockSpec((panels, block, b), lambda i: (0, i, 0)),
        ],
        out_specs=pl.BlockSpec((panels * b, cols), lambda i: (0, 0)),
        out_shape=jax.ShapeDtypeStruct((panels * b, cols), f32),
        compiler_params=pltpu.CompilerParams(vmem_limit_bytes=VMEM_LIMIT),
        name="product",
    )(a, v)


def sum_rows(mine, other):
    wide, cols = mine.shape

    def kernel(mine_ref, other_ref, sum_ref, z_ref):
        total = mine_ref[...] + other_ref[...]
        sum_ref[...] = total
        z_ref[...] = total.T

    return pl.pallas_call(
        kernel,
        out_shape=(jax.ShapeDtypeStruct((wide, cols), f32), jax.ShapeDtypeStruct((cols, wide), f32)),
        compiler_params=pltpu.CompilerParams(vmem_limit_bytes=VMEM_LIMIT),
        name="sum_rows",
    )(mine, other)


def gram_kernel(v_ref, z_ref, out_ref, cross_ref):
    @pl.when(pl.program_id(0) == 0)
    def _():
        out_ref[...] = jnp.zeros_like(out_ref)
        cross_ref[...] = jnp.zeros_like(cross_ref)

    v = jnp.concatenate([v_ref[p] for p in range(v_ref.shape[0])], axis=1)
    vt_hi, vt_lo = split(v.T)
    v_hi, v_lo = split(v)
    z_hi, z_lo = split(z_ref[...])
    b = v_ref.shape[2]
    out_ref[...] += dot(vt_hi, z_hi) + (dot(vt_lo, z_hi) + dot(vt_hi, z_lo))
    cross_ref[...] += dot(vt_hi[:b], v_hi[:, b:]) + (dot(vt_lo[:b], v_hi[:, b:]) + dot(vt_hi[:b], v_lo[:, b:]))


def gram(v, z):
    panels, rows, b = v.shape
    wide = panels * b
    block = row_block(rows)
    return pl.pallas_call(
        gram_kernel,
        grid=(rows // block,),
        in_specs=[
            pl.BlockSpec((panels, block, b), lambda i: (0, i, 0)),
            pl.BlockSpec((block, wide), lambda i: (i, 0)),
        ],
        out_specs=[
            pl.BlockSpec((wide, wide), lambda i: (0, 0)),
            pl.BlockSpec((b, b), lambda i: (0, 0)),
        ],
        out_shape=(jax.ShapeDtypeStruct((wide, wide), f32), jax.ShapeDtypeStruct((b, b), f32)),
        compiler_params=pltpu.CompilerParams(vmem_limit_bytes=VMEM_LIMIT),
        name="gram",
    )(v, z)


def factor_kernel(t_ref, m_ref, n_ref, zt_ref, vc_ref, hi_ref, lo_ref):
    b = t_ref.shape[1]
    upper = lax.broadcasted_iota(jnp.int32, (b, b), 0) <= lax.broadcasted_iota(jnp.int32, (b, b), 1)
    t1 = jnp.where(upper, t_ref[0], 0.0)
    t2 = jnp.where(upper, t_ref[1], 0.0)
    n = n_ref[...]
    m11, m12, m22 = m_ref[:b, :b], m_ref[:b, b:], m_ref[b:, b:]
    k1 = exact(t1.T, exact(m11, t1))
    e = exact(t1.T, m12) - 0.5 * exact(k1.T, n)
    nte = exact(n.T, e)
    k2 = exact(t2.T, exact(m22 - nte - nte.T, t2))
    s12 = -exact(t1, exact(n, t2))
    r11 = -0.5 * k1
    r12 = exact(0.5 * exact(k1, n) - e, t2)
    r22 = -0.5 * k2
    s = jnp.concatenate([jnp.concatenate([t1, s12], 1), jnp.concatenate([jnp.zeros_like(t1), t2], 1)], 0)
    r = jnp.concatenate([jnp.concatenate([r11 + r11.T, r12], 1), jnp.concatenate([r12.T, r22 + r22.T], 1)], 0)
    vct = vc_ref[...].T
    pt = exact(s.T, zt_ref[...]) + exact(r, vct)
    qt = exact(s, vct)
    wide = 2 * b
    hi_ref[:wide], lo_ref[:wide] = split(pt)
    hi_ref[wide:], lo_ref[wide:] = split(qt)


def factors(tfactor, m, n, zt, vc):
    wide, cols = zt.shape
    out = jax.ShapeDtypeStruct((2 * wide, cols), bf16)
    return pl.pallas_call(
        factor_kernel,
        out_shape=(out, out),
        compiler_params=pltpu.CompilerParams(vmem_limit_bytes=VMEM_LIMIT),
        name="factors",
    )(tfactor, m, n, zt, vc)


def update_kernel(a_ref, v_ref, z_ref, hi_ref, lo_ref, out_ref):
    left = jnp.concatenate([v_ref[p] for p in range(v_ref.shape[0])] + [z_ref[...]], axis=1)
    l_hi, l_lo = split(left)
    hi = hi_ref[...]
    out_ref[...] = a_ref[...] - (dot(l_hi, hi) + (dot(l_lo, hi) + dot(l_hi, lo_ref[...])))


def update(a, v, z, hi, lo):
    rows, cols = a.shape
    panels, _, b = v.shape
    block = row_block(rows)
    wide = panels * b
    return pl.pallas_call(
        update_kernel,
        grid=(rows // block,),
        in_specs=[
            pl.BlockSpec((block, cols), lambda i: (i, 0)),
            pl.BlockSpec((panels, block, b), lambda i: (0, i, 0)),
            pl.BlockSpec((block, wide), lambda i: (i, 0)),
            pl.BlockSpec((2 * wide, cols), lambda i: (0, 0)),
            pl.BlockSpec((2 * wide, cols), lambda i: (0, 0)),
        ],
        out_specs=pl.BlockSpec((block, cols), lambda i: (i, 0)),
        out_shape=jax.ShapeDtypeStruct((rows, cols), f32),
        compiler_params=pltpu.CompilerParams(vmem_limit_bytes=VMEM_LIMIT),
        name="update",
    )(a, v, z, hi, lo)


def row_sum(value):
    total = lax.axis_size("row")
    if total == 2:
        return lax.ppermute(value, "row", [(0, 1), (1, 0)])
    return lax.psum(value, "row") - value


def general_body(matrix, vectors, tfactor):
    rows_here, cols_here = matrix.shape
    own = vectors.shape[1]
    row_total, col_total = lax.axis_size("row"), lax.axis_size("col")
    row, col = lax.axis_index("row"), lax.axis_index("col")
    owner = col * row_total // col_total
    offset = col * cols_here - owner * rows_here

    v_rows = lax.all_gather(vectors, "col", axis=1, tiled=True)
    mine = lax.dynamic_slice_in_dim(v_rows, offset, cols_here, 1)
    v_cols = mine
    for shift in range(1, row_total):
        other = lax.ppermute(mine, "row", [(i, (i + shift) % row_total) for i in range(row_total)])
        v_cols = jnp.where((row - owner) % row_total == shift, other, v_cols)

    part = product(matrix, v_rows)
    zt, z = sum_rows(part, row_sum(part))

    per_row = col_total // row_total
    z_own = None
    for piece in range(row_total):
        pairs = []
        for r in range(row_total):
            for c in range(per_row):
                pairs.append((r * col_total + r * per_row + c, r * col_total + c * row_total + piece))
        sent = lax.ppermute(z[piece * own : (piece + 1) * own], ("row", "col"), pairs)
        z_own = sent if z_own is None else z_own + sent
    z_rows = lax.all_gather(z_own, "col", axis=0, tiled=True)

    m, n = gram(v_rows, z_rows)
    small = jnp.concatenate([m, jnp.concatenate([n, jnp.zeros_like(n)], 1)], 0)
    small = small + row_sum(small)
    b = n.shape[0]
    v_pair = jnp.concatenate([v_cols[0], v_cols[1]], axis=1)
    hi, lo = factors(tfactor, small[: 2 * b], small[2 * b :, :b], zt, v_pair)
    return update(matrix, v_rows, z_rows, hi, lo)


def ring_chip(position, chips):
    position %= chips
    return 2 * position if position < chips // 2 else 2 * (chips - 1 - position) + 1


def ring_chips_here(chips, steps):
    chip = lax.axis_index("col") // 2
    place = jnp.where(chip % 2 == 0, chip // 2, chips - 1 - chip // 2)

    def at(position):
        position = position % chips
        return jnp.where(position < chips // 2, 2 * position, 2 * (chips - 1 - position) + 1)

    core = lax.axis_index("col") % 2
    signs = 2 * core - 1
    return [at(place + signs * step) for step in steps], [at(place - signs * step) for step in steps]


def after(value, *others):
    if not others:
        return value
    vmem = pl.BlockSpec(memory_space=pltpu.VMEM)

    def kernel(*refs):
        refs[-1][...] = refs[0][...]

    return pl.pallas_call(
        kernel,
        in_specs=[vmem] * (1 + len(others)),
        out_specs=vmem,
        out_shape=jax.ShapeDtypeStruct(value.shape, value.dtype),
        compiler_params=pltpu.CompilerParams(vmem_limit_bytes=VMEM_LIMIT),
        name="after",
    )(value, *others)


def joined(mine):
    core = lax.axis_index("col") % 2
    other = lax.ppermute(mine, "col", [(c, c ^ 1) for c in range(lax.axis_size("col"))])
    first, second = jnp.where(core == 0, mine, other), jnp.where(core == 0, other, mine)
    return jnp.concatenate([first, second], axis=0)


def ring_gather(own_block, work):
    chips = lax.axis_size("col") // 2
    core = lax.axis_index("col") % 2
    swap = [(c, c ^ 1) for c in range(2 * chips)]
    around = []
    for i in range(chips):
        around.append((2 * ring_chip(i, chips), 2 * ring_chip(i + 1, chips)))
        around.append((2 * ring_chip(i, chips) + 1, 2 * ring_chip(i - 1, chips) + 1))

    held = own_block
    blocks = [held]
    for step in range(1, chips // 2 + 1):
        if step == chips // 2:
            rows = held.shape[0] // 2
            held = lax.dynamic_slice_in_dim(held, core * rows, rows, 0)
        came = lax.ppermute(held, "col", around)
        held = after(came, *work(step - 1, blocks))
        if step < chips // 2:
            blocks = [held, lax.ppermute(held, "col", swap)]
    work(chips // 2, [joined(held)])


def ring_order(chips):
    came, other = ring_chips_here(chips, range(chips // 2 + 1))
    order = [came[0]]
    for step in range(1, chips // 2):
        order += [came[step], other[step]]
    return order + [came[chips // 2]]


def part_kernel(count, first, index_ref, a_ref, *refs):
    values, refs = refs[:count], refs[count:]
    if first:
        out_ref, v_ref, cross_ref = refs
    else:
        total_ref, _, sum_ref, out_ref, v_ref, cross_ref = refs
    step = pl.program_id(0)

    @pl.when(step == 0)
    def _():
        out_ref[...] = jnp.zeros_like(out_ref) if first else total_ref[...]
        cross_ref[...] = jnp.zeros_like(cross_ref) if first else sum_ref[...]

    for j in range(count):

        @pl.when(step == j)
        def _(j=j):
            v_ref[...] = values[j][...]

    v_hi, v_lo = split(v_ref[...].T)
    a_hi, a_lo = split(a_ref[...])
    wide = v_hi.shape[0]
    both = dot(jnp.concatenate([v_hi, v_lo], axis=0), a_hi)
    out_ref[...] += both[:wide] + (both[wide:] + dot(v_hi, a_lo))
    b = wide // 2
    w_hi, w_lo = split(v_ref[:, b:])
    cross_ref[...] += dot(v_hi[:b], w_hi) + (dot(v_lo[:b], w_hi) + dot(v_hi[:b], w_lo))


def part_product(a, blocks, index, state):
    rows, cols = a.shape
    block, wide = blocks[0].shape
    count = len(blocks)
    first = state is None
    whole = pl.BlockSpec(memory_space=pltpu.VMEM)
    total = pl.BlockSpec((wide, cols), lambda i, index: (0, 0))
    in_specs = [pl.BlockSpec((block, cols), lambda i, index: (index[i], 0))] + [whole] * count
    operands = list(blocks)
    aliases = {}
    cross = pl.BlockSpec((wide // 2, wide // 2), lambda i, index: (0, 0))
    if not first:
        in_specs += [total, pl.BlockSpec(memory_space=pl.ANY), cross]
        operands += list(state)
        aliases = {2 + count: 0, 3 + count: 1}
    return pl.pallas_call(
        functools.partial(part_kernel, count, first),
        grid_spec=pltpu.PrefetchScalarGridSpec(
            num_scalar_prefetch=1,
            grid=(count,),
            in_specs=in_specs,
            out_specs=[total, pl.BlockSpec((block, wide), lambda i, index: (index[i], 0)), cross],
        ),
        out_shape=(
            jax.ShapeDtypeStruct((wide, cols), f32),
            jax.ShapeDtypeStruct((rows, wide), f32),
            jax.ShapeDtypeStruct((wide // 2, wide // 2), f32),
        ),
        input_output_aliases=aliases,
        cost_estimate=cost(6 * count * block * cols * wide, 4 * count * block * (cols + 2 * wide)),
        compiler_params=pltpu.CompilerParams(vmem_limit_bytes=VMEM_LIMIT),
        name="part_product",
    )(index, a, *operands)


def own_gram_kernel(index_ref, v_ref, z_ref, out_ref):
    out_ref[...] = exact(v_ref[...].T, z_ref[...])


def own_gram(index, v, z):
    rows, wide = z.shape
    b = wide // 2
    return pl.pallas_call(
        own_gram_kernel,
        grid_spec=pltpu.PrefetchScalarGridSpec(
            num_scalar_prefetch=1,
            grid=(1,),
            in_specs=[
                pl.BlockSpec((rows, b), lambda i, index: (index[0], index[1])),
                pl.BlockSpec((rows, wide), lambda i, index: (0, 0)),
            ],
            out_specs=pl.BlockSpec((b, wide), lambda i, index: (0, 0)),
        ),
        out_shape=jax.ShapeDtypeStruct((b, wide), f32),
        compiler_params=pltpu.CompilerParams(vmem_limit_bytes=VMEM_LIMIT),
        name="own_gram",
    )(index, v, z)


def part_update_kernel(count, first, index_ref, a_ref, v_ref, hi_ref, lo_ref, *refs):
    values, (out_ref, token_ref) = refs[:count], refs[-2:]
    step = pl.program_id(0)
    token_ref[...] = jnp.zeros_like(token_ref)
    hi, lo = hi_ref[...], lo_ref[...]
    for j in range(count):

        @pl.when(step == j)
        def _(j=j):
            left = jnp.concatenate([v_ref[...], values[j][...]], axis=1)
            l_hi, l_lo = split(left)
            out_ref[...] = a_ref[...] - (dot(l_hi, hi) + (dot(l_lo, hi) + dot(l_hi, lo)))


def part_update(a, v, hi, lo, blocks, index, state):
    rows, cols = a.shape
    wide = v.shape[1]
    count = len(blocks)
    block = blocks[0].shape[0]
    first = state is None
    placed = lambda i, index: (index[i], 0)
    in_specs = [
        pl.BlockSpec((block, cols), placed),
        pl.BlockSpec((block, wide), placed),
    ] + [pl.BlockSpec(memory_space=pltpu.VMEM)] * (2 + count)
    operands = [a, v, hi, lo] + list(blocks)
    aliases = {}
    if not first:
        in_specs.append(pl.BlockSpec(memory_space=pl.ANY))
        operands.append(state)
        aliases = {len(operands): 0}
    return pl.pallas_call(
        functools.partial(part_update_kernel, count, first),
        grid_spec=pltpu.PrefetchScalarGridSpec(
            num_scalar_prefetch=1,
            grid=(count,),
            in_specs=in_specs,
            out_specs=[pl.BlockSpec((block, cols), placed), TOKEN_SPEC],
        ),
        out_shape=(jax.ShapeDtypeStruct((rows, cols), f32), TOKEN),
        input_output_aliases=aliases,
        cost_estimate=cost(12 * count * block * cols * wide, 4 * count * block * (2 * cols + 2 * wide)),
        compiler_params=pltpu.CompilerParams(vmem_limit_bytes=VMEM_LIMIT),
        name="part_update",
    )(index, *operands)


def quad_sum(value, axis_1, bit_1, axis_2, bit_2):
    size_1, size_2 = lax.axis_size(axis_1), lax.axis_size(axis_2)
    if axis_1 == axis_2:
        pairs = [[(c, c ^ bits) for c in range(size_1)] for bits in (bit_1, bit_2, bit_1 | bit_2)]
        parts = [lax.ppermute(value, axis_1, pair) for pair in pairs]
    else:
        first = [(c, c ^ bit_1) for c in range(size_1)]
        second = [(c, c ^ bit_2) for c in range(size_2)]
        diagonal = [(r * size_2 + c, (r ^ bit_1) * size_2 + (c ^ bit_2)) for r in range(size_1) for c in range(size_2)]
        parts = [lax.ppermute(value, axis_1, first), lax.ppermute(value, axis_2, second)]
        parts.append(lax.ppermute(value, (axis_1, axis_2), diagonal))
    return (value + parts[0]) + (parts[1] + parts[2])


def rest_sum(value):
    cols, bit = lax.axis_size("col"), 4
    while bit * 2 < cols:
        value = quad_sum(value, "col", bit, "col", 2 * bit)
        bit *= 4
    if bit < cols:
        value = value + lax.ppermute(value, "col", [(c, c ^ bit) for c in range(cols)])
    return value


def whole_sum(value):
    core = lax.axis_index("col") % 2
    other = lax.ppermute(value, "col", [(c, c ^ 1) for c in range(lax.axis_size("col"))])
    return jnp.concatenate([jnp.where(core == 0, value, other), jnp.where(core == 0, other, value)], axis=0)


def body(matrix, vectors, tfactor):
    rows_here, cols_here = matrix.shape
    own, b = vectors.shape[1:]
    cols = lax.axis_size("col")
    row, col = lax.axis_index("row"), lax.axis_index("col")
    chips = cols // 2
    half = chips // 2
    chip, core = col // 2, col % 2
    both = ("row", "col")

    order = ring_order(chips)
    last = chips // 2

    def chips_of(step):
        return order[:1] if step == 0 else order[2 * step - 1 : 2 * step + 1]

    owner = col // chips
    across = [(0, 1), (1, 0)]
    state = None

    def multiply(step, blocks):
        nonlocal state
        here = chips_of(step)
        state = part_product(matrix, blocks, jnp.stack(here).astype(jnp.int32), state)
        return [state[2]]

    ring_gather(joined(jnp.concatenate([vectors[0], vectors[1]], axis=1)), multiply)
    part, v_rows, cross = state

    def at(r, j, k):
        return r * cols + 2 * (j % chips) + k

    homes = [(r, j) for r in range(2) for j in range(r * half, (r + 1) * half)]
    along = [(at(r, j, 1), at(r, j + half, 1)) for r, j in homes]
    direct = [(at(1 - r, j, 1), at(r, j + half, 1)) for r, j in homes]
    across = [(0, 1), (1, 0)]
    across = [(0, 1), (1, 0)]
    outward = [(at(r, j, k), at(1 - r, j, k)) for r, j in homes for k in range(2)]
    inward = [(at(1 - r, j, k), at(r, j, k)) for r, j in homes for k in range(2)]
    home = owner == row
    given2 = lax.ppermute(part, both, direct)
    given1 = lax.ppermute(part, both, along)
    kept = lax.ppermute(part, both, inward)
    mine = lax.dynamic_slice_in_dim(v_rows, (col - owner * chips) * cols_here, cols_here, 0)
    sent = lax.ppermute(mine, both, outward)
    cross = cross + lax.ppermute(cross, "row", across)
    kept = after(kept, sent, cross)
    kept_rest = lax.ppermute(after(part, kept), both, outward)
    z = jnp.where(home, part + kept, given1 + given2).T
    z = jnp.where(home == (core == 0), z, lax.ppermute(z, "col", [(c, c ^ 1) for c in range(cols)]))
    v_cols = jnp.where(home, mine, sent)

    def z_index(j):
        return 2 * (j % half) + jnp.where(j // half == row, 0, 1)

    out = None
    waiting = []
    sums = [own_gram(jnp.stack([z_index(chip), core]).astype(jnp.int32), v_rows, z)]

    def subtract(step, blocks):
        nonlocal out
        waiting.extend(zip(chips_of(step), blocks))
        if step == 0:
            sums.append(quad_sum(sums[-1], "row", 1, "col", 2))
            return sums[-1:]
        if step == 1:
            sums.append(rest_sum(sums[-1]))
            return sums[-1:]
        if step < last - 1:
            return []
        if step == last - 1:
            zt = part + (kept + after(kept_rest, sums[1]))
            sums.extend(factors(tfactor, whole_sum(sums[-1]), cross, zt, v_cols))
        ready, waiting[:] = (waiting[:-2], waiting[-2:]) if step < last else (waiting[:], [])
        index = jnp.stack([z_index(j) for j, _ in ready]).astype(jnp.int32)
        out, token = part_update(matrix, v_rows, *sums[-2:], [block for _, block in ready], index, out)
        return [token]

    ring_gather(z, subtract)
    return out


def solution(mesh):
    rows, cols = mesh.shape["row"], mesh.shape["col"]
    pairs = rows == 2 and cols >= 8 and cols & (cols - 1) == 0
    return jax.shard_map(
        body if pairs else general_body,
        mesh=mesh,
        in_specs=(P("row", "col"), P(None, ("row", "col"), None), P()),
        out_specs=P("row", "col"),
        check_vma=False,
    )
```

```python
import functools

import jax
import jax.numpy as jnp
from jax import lax
from jax.experimental import pallas as pl
from jax.experimental.pallas import tpu as pltpu
from jax.sharding import PartitionSpec as P

highest = lax.Precision.HIGHEST
f32 = jnp.float32
bf16 = jnp.bfloat16
VMEM_LIMIT = 48 * 1024 * 1024


def split(value):
    high = value.astype(bf16)
    low = (value - high.astype(f32)).astype(bf16)
    return high, low


def dot(left, right):
    return jnp.dot(left, right, preferred_element_type=f32)


def exact(left, right):
    return jnp.dot(left, right, precision=highest, preferred_element_type=f32)


def exact_nt(left, right):
    return lax.dot_general(left, right, (((1,), (1,)), ((), ())), precision=highest, preferred_element_type=f32)


def cost(flops, count):
    return pl.CostEstimate(flops=flops, bytes_accessed=count, transcendentals=0)


def row_block(rows):
    return min(rows, 512)


def product_kernel(a_ref, v_ref, out_ref):
    @pl.when(pl.program_id(0) == 0)
    def _():
        out_ref[...] = jnp.zeros_like(out_ref)

    v = jnp.concatenate([v_ref[p] for p in range(v_ref.shape[0])], axis=1)
    v_hi, v_lo = split(v.T)
    a_hi, a_lo = split(a_ref[...])
    wide = v_hi.shape[0]
    both = dot(jnp.concatenate([v_hi, v_lo], axis=0), a_hi)
    out_ref[...] += both[:wide] + (both[wide:] + dot(v_hi, a_lo))


def product(a, v):
    rows, cols = a.shape
    panels, _, b = v.shape
    block = row_block(rows)
    return pl.pallas_call(
        product_kernel,
        grid=(rows // block,),
        in_specs=[
            pl.BlockSpec((block, cols), lambda i: (i, 0)),
            pl.BlockSpec((panels, block, b), lambda i: (0, i, 0)),
        ],
        out_specs=pl.BlockSpec((panels * b, cols), lambda i: (0, 0)),
        out_shape=jax.ShapeDtypeStruct((panels * b, cols), f32),
        compiler_params=pltpu.CompilerParams(vmem_limit_bytes=VMEM_LIMIT),
        name="product",
    )(a, v)


def sum_rows(mine, other):
    wide, cols = mine.shape

    def kernel(mine_ref, other_ref, sum_ref, z_ref):
        total = mine_ref[...] + other_ref[...]
        sum_ref[...] = total
        z_ref[...] = total.T

    return pl.pallas_call(
        kernel,
        out_shape=(jax.ShapeDtypeStruct((wide, cols), f32), jax.ShapeDtypeStruct((cols, wide), f32)),
        compiler_params=pltpu.CompilerParams(vmem_limit_bytes=VMEM_LIMIT),
        name="sum_rows",
    )(mine, other)


def gram_kernel(v_ref, z_ref, out_ref, cross_ref):
    @pl.when(pl.program_id(0) == 0)
    def _():
        out_ref[...] = jnp.zeros_like(out_ref)
        cross_ref[...] = jnp.zeros_like(cross_ref)

    v = jnp.concatenate([v_ref[p] for p in range(v_ref.shape[0])], axis=1)
    vt_hi, vt_lo = split(v.T)
    v_hi, v_lo = split(v)
    z_hi, z_lo = split(z_ref[...])
    b = v_ref.shape[2]
    out_ref[...] += dot(vt_hi, z_hi) + (dot(vt_lo, z_hi) + dot(vt_hi, z_lo))
    cross_ref[...] += dot(vt_hi[:b], v_hi[:, b:]) + (dot(vt_lo[:b], v_hi[:, b:]) + dot(vt_hi[:b], v_lo[:, b:]))


def gram(v, z):
    panels, rows, b = v.shape
    wide = panels * b
    block = row_block(rows)
    return pl.pallas_call(
        gram_kernel,
        grid=(rows // block,),
        in_specs=[
            pl.BlockSpec((panels, block, b), lambda i: (0, i, 0)),
            pl.BlockSpec((block, wide), lambda i: (i, 0)),
        ],
        out_specs=[
            pl.BlockSpec((wide, wide), lambda i: (0, 0)),
            pl.BlockSpec((b, b), lambda i: (0, 0)),
        ],
        out_shape=(jax.ShapeDtypeStruct((wide, wide), f32), jax.ShapeDtypeStruct((b, b), f32)),
        compiler_params=pltpu.CompilerParams(vmem_limit_bytes=VMEM_LIMIT),
        name="gram",
    )(v, z)


def factor_kernel(t_ref, m_ref, n_ref, zt_ref, vc_ref, hi_ref, lo_ref):
    b = t_ref.shape[1]
    upper = lax.broadcasted_iota(jnp.int32, (b, b), 0) <= lax.broadcasted_iota(jnp.int32, (b, b), 1)
    t1 = jnp.where(upper, t_ref[0], 0.0)
    t2 = jnp.where(upper, t_ref[1], 0.0)
    n = n_ref[...]
    m11, m12, m22 = m_ref[:b, :b], m_ref[:b, b:], m_ref[b:, b:]
    k1 = exact(t1.T, exact(m11, t1))
    e = exact(t1.T, m12) - 0.5 * exact(k1.T, n)
    nte = exact(n.T, e)
    k2 = exact(t2.T, exact(m22 - nte - nte.T, t2))
    s12 = -exact(t1, exact(n, t2))
    r11 = -0.5 * k1
    r12 = exact(0.5 * exact(k1, n) - e, t2)
    r22 = -0.5 * k2
    s = jnp.concatenate([jnp.concatenate([t1, s12], 1), jnp.concatenate([jnp.zeros_like(t1), t2], 1)], 0)
    r = jnp.concatenate([jnp.concatenate([r11 + r11.T, r12], 1), jnp.concatenate([r12.T, r22 + r22.T], 1)], 0)
    vct = jnp.concatenate([vc_ref[0], vc_ref[1]], axis=1).T
    pt = exact(s.T, zt_ref[...]) + exact(r, vct)
    qt = exact(s, vct)
    wide = 2 * b
    hi_ref[:wide], lo_ref[:wide] = split(pt)
    hi_ref[wide:], lo_ref[wide:] = split(qt)


def factors(tfactor, m, n, zt, vc):
    wide, cols = zt.shape
    out = jax.ShapeDtypeStruct((2 * wide, cols), bf16)
    return pl.pallas_call(
        factor_kernel,
        out_shape=(out, out),
        compiler_params=pltpu.CompilerParams(vmem_limit_bytes=VMEM_LIMIT),
        name="factors",
    )(tfactor, m, n, zt, vc)


def update_kernel(a_ref, v_ref, z_ref, hi_ref, lo_ref, out_ref):
    left = jnp.concatenate([v_ref[p] for p in range(v_ref.shape[0])] + [z_ref[...]], axis=1)
    l_hi, l_lo = split(left)
    hi = hi_ref[...]
    out_ref[...] = a_ref[...] - (dot(l_hi, hi) + (dot(l_lo, hi) + dot(l_hi, lo_ref[...])))


def update(a, v, z, hi, lo):
    rows, cols = a.shape
    panels, _, b = v.shape
    block = row_block(rows)
    wide = panels * b
    return pl.pallas_call(
        update_kernel,
        grid=(rows // block,),
        in_specs=[
            pl.BlockSpec((block, cols), lambda i: (i, 0)),
            pl.BlockSpec((panels, block, b), lambda i: (0, i, 0)),
            pl.BlockSpec((block, wide), lambda i: (i, 0)),
            pl.BlockSpec((2 * wide, cols), lambda i: (0, 0)),
            pl.BlockSpec((2 * wide, cols), lambda i: (0, 0)),
        ],
        out_specs=pl.BlockSpec((block, cols), lambda i: (i, 0)),
        out_shape=jax.ShapeDtypeStruct((rows, cols), f32),
        compiler_params=pltpu.CompilerParams(vmem_limit_bytes=VMEM_LIMIT),
        name="update",
    )(a, v, z, hi, lo)


def row_sum(value):
    total = lax.axis_size("row")
    if total == 2:
        return lax.ppermute(value, "row", [(0, 1), (1, 0)])
    return lax.psum(value, "row") - value


def general_body(matrix, vectors, tfactor):
    rows_here, cols_here = matrix.shape
    own = vectors.shape[1]
    row_total, col_total = lax.axis_size("row"), lax.axis_size("col")
    row, col = lax.axis_index("row"), lax.axis_index("col")
    owner = col * row_total // col_total
    offset = col * cols_here - owner * rows_here

    v_rows = lax.all_gather(vectors, "col", axis=1, tiled=True)
    mine = lax.dynamic_slice_in_dim(v_rows, offset, cols_here, 1)
    v_cols = mine
    for shift in range(1, row_total):
        other = lax.ppermute(mine, "row", [(i, (i + shift) % row_total) for i in range(row_total)])
        v_cols = jnp.where((row - owner) % row_total == shift, other, v_cols)

    part = product(matrix, v_rows)
    zt, z = sum_rows(part, row_sum(part))

    per_row = col_total // row_total
    z_own = None
    for piece in range(row_total):
        pairs = []
        for r in range(row_total):
            for c in range(per_row):
                pairs.append((r * col_total + r * per_row + c, r * col_total + c * row_total + piece))
        sent = lax.ppermute(z[piece * own : (piece + 1) * own], ("row", "col"), pairs)
        z_own = sent if z_own is None else z_own + sent
    z_rows = lax.all_gather(z_own, "col", axis=0, tiled=True)

    m, n = gram(v_rows, z_rows)
    small = jnp.concatenate([m, jnp.concatenate([n, jnp.zeros_like(n)], 1)], 0)
    small = small + row_sum(small)
    b = n.shape[0]
    hi, lo = factors(tfactor, small[: 2 * b], small[2 * b :, :b], zt, v_cols)
    return update(matrix, v_rows, z_rows, hi, lo)


def ring_chip(position, chips):
    position %= chips
    return 2 * position if position < chips // 2 else 2 * (chips - 1 - position) + 1


def ring_chips_here(chips, steps):
    chip = lax.axis_index("col") // 2
    place = jnp.where(chip % 2 == 0, chip // 2, chips - 1 - chip // 2)

    def at(position):
        position = position % chips
        return jnp.where(position < chips // 2, 2 * position, 2 * (chips - 1 - position) + 1)

    core = lax.axis_index("col") % 2
    signs = 2 * core - 1
    return [at(place + signs * step) for step in steps], [at(place - signs * step) for step in steps]


def ring_gather(streams):
    chips = lax.axis_size("col") // 2
    core = lax.axis_index("col") % 2
    swap = [(c, c ^ 1) for c in range(2 * chips)]
    around = []
    for i in range(chips):
        around.append((2 * ring_chip(i, chips), 2 * ring_chip(i + 1, chips)))
        around.append((2 * ring_chip(i, chips) + 1, 2 * ring_chip(i - 1, chips) + 1))

    def joined(mine):
        other = lax.ppermute(mine, "col", swap)
        first, second = jnp.where(core == 0, mine, other), jnp.where(core == 0, other, mine)
        return jnp.concatenate([first, second], axis=0)

    held = [joined(mine) for mine in streams]
    result = [[block] for block in held]
    for _ in range(1, chips // 2):
        held = [lax.ppermute(block, "col", around) for block in held]
        for blocks, block in zip(result, held):
            blocks += [block, lax.ppermute(block, "col", swap)]
    for blocks, block in zip(result, held):
        rows = block.shape[0] // 2
        part = lax.dynamic_slice_in_dim(block, core * rows, rows, 0)
        blocks.append(joined(lax.ppermute(part, "col", around)))
    return result


def after(value, *others):
    if not others:
        return value
    vmem = pl.BlockSpec(memory_space=pltpu.VMEM)

    def kernel(*refs):
        refs[-1][...] = refs[0][...]

    return pl.pallas_call(
        kernel,
        in_specs=[vmem] * (1 + len(others)),
        out_specs=vmem,
        out_shape=jax.ShapeDtypeStruct(value.shape, value.dtype),
        compiler_params=pltpu.CompilerParams(vmem_limit_bytes=VMEM_LIMIT),
        name="after",
    )(value, *others)


def chip_block(mine):
    core = lax.axis_index("col") % 2
    other = lax.ppermute(mine, "col", [(c, c ^ 1) for c in range(lax.axis_size("col"))])
    first, second = jnp.where(core == 0, mine, other), jnp.where(core == 0, other, mine)
    return jnp.concatenate([first, second], axis=0)


def ring_work(own_block, work):
    chips = lax.axis_size("col") // 2
    core = lax.axis_index("col") % 2
    swap = [(c, c ^ 1) for c in range(2 * chips)]
    around = []
    for i in range(chips):
        around.append((2 * ring_chip(i, chips), 2 * ring_chip(i + 1, chips)))
        around.append((2 * ring_chip(i, chips) + 1, 2 * ring_chip(i - 1, chips) + 1))

    held = own_block
    blocks = [held]
    for step in range(1, chips // 2 + 1):
        if step == chips // 2:
            rows = held.shape[0] // 2
            held = lax.dynamic_slice_in_dim(held, core * rows, rows, 0)
        came = lax.ppermute(held, "col", around)
        held = after(came, *work(step - 1, blocks))
        if step < chips // 2:
            blocks = [held, lax.ppermute(held, "col", swap)]
    work(chips // 2, [chip_block(held)])


def ring_order(chips):
    came, other = ring_chips_here(chips, range(chips // 2 + 1))
    order = [came[0]]
    for step in range(1, chips // 2):
        order += [came[step], other[step]]
    return order + [came[chips // 2]]


def part_kernel(count, first, index_ref, a_ref, *refs):
    values, refs = refs[:count], refs[count:]
    if first:
        out_ref, v_ref, cross_ref = refs
    else:
        total_ref, _, sum_ref, out_ref, v_ref, cross_ref = refs
    step = pl.program_id(0)

    @pl.when(step == 0)
    def _():
        out_ref[...] = jnp.zeros_like(out_ref) if first else total_ref[...]
        cross_ref[...] = jnp.zeros_like(cross_ref) if first else sum_ref[...]

    for j in range(count):

        @pl.when(step == j)
        def _(j=j):
            v_ref[...] = values[j][...]

    v_hi, v_lo = split(v_ref[...].T)
    a_hi, a_lo = split(a_ref[...])
    wide = v_hi.shape[0]
    both = dot(jnp.concatenate([v_hi, v_lo], axis=0), a_hi)
    out_ref[...] += both[:wide] + (both[wide:] + dot(v_hi, a_lo))
    b = wide // 2
    w_hi, w_lo = split(v_ref[:, b:])
    cross_ref[...] += dot(v_hi[:b], w_hi) + (dot(v_lo[:b], w_hi) + dot(v_hi[:b], w_lo))


def part_product(a, blocks, index, state):
    rows, cols = a.shape
    block, wide = blocks[0].shape
    count = len(blocks)
    first = state is None
    whole = pl.BlockSpec(memory_space=pltpu.VMEM)
    total = pl.BlockSpec((wide, cols), lambda i, index: (0, 0))
    in_specs = [pl.BlockSpec((block, cols), lambda i, index: (index[i], 0))] + [whole] * count
    operands = list(blocks)
    aliases = {}
    cross = pl.BlockSpec((wide // 2, wide // 2), lambda i, index: (0, 0))
    if not first:
        in_specs += [total, pl.BlockSpec(memory_space=pl.ANY), cross]
        operands += list(state)
        aliases = {2 + count: 0, 3 + count: 1}
    return pl.pallas_call(
        functools.partial(part_kernel, count, first),
        grid_spec=pltpu.PrefetchScalarGridSpec(
            num_scalar_prefetch=1,
            grid=(count,),
            in_specs=in_specs,
            out_specs=[total, pl.BlockSpec((block, wide), lambda i, index: (index[i], 0)), cross],
        ),
        out_shape=(
            jax.ShapeDtypeStruct((wide, cols), f32),
            jax.ShapeDtypeStruct((rows, wide), f32),
            jax.ShapeDtypeStruct((wide // 2, wide // 2), f32),
        ),
        input_output_aliases=aliases,
        cost_estimate=cost(6 * count * block * cols * wide, 4 * count * block * (cols + 2 * wide)),
        compiler_params=pltpu.CompilerParams(vmem_limit_bytes=VMEM_LIMIT),
        name="part_product",
    )(index, a, *operands)


def own_gram_kernel(index_ref, v_ref, z1_ref, z2_ref, out_ref):
    b = z1_ref.shape[1]
    v = v_ref[...]
    vt = v.T
    z = jnp.concatenate([z1_ref[...], z2_ref[...]], axis=1)
    out_ref[:b] = exact(vt[:b], z)
    out_ref[b:, :b] = exact(vt[:b], v[:, b:])
    out_ref[b:, b:] = exact(vt[b:], z[:, b:])


def own_gram(index, v, z1, z2):
    rows, b = z1.shape
    return pl.pallas_call(
        own_gram_kernel,
        grid_spec=pltpu.PrefetchScalarGridSpec(
            num_scalar_prefetch=1,
            grid=(1,),
            in_specs=[
                pl.BlockSpec((rows, 2 * b), lambda i, index: (index[0], 0)),
                pl.BlockSpec((rows, b), lambda i, index: (0, 0)),
                pl.BlockSpec((rows, b), lambda i, index: (0, 0)),
            ],
            out_specs=pl.BlockSpec((2 * b, 2 * b), lambda i, index: (0, 0)),
        ),
        out_shape=jax.ShapeDtypeStruct((2 * b, 2 * b), f32),
        compiler_params=pltpu.CompilerParams(vmem_limit_bytes=VMEM_LIMIT),
        name="own_gram",
    )(index, v, z1, z2)


def part_update_kernel(count, first, index_ref, a_ref, v_ref, hi_ref, lo_ref, *refs):
    values, out_ref = refs[: 2 * count], refs[-1]
    step = pl.program_id(0)
    rows = a_ref.shape[0]
    hi, lo = hi_ref[...], lo_ref[...]
    for j in range(2 * count):

        @pl.when(step == j)
        def _(j=j):
            here = pl.ds((j % 2) * rows, rows)
            left = jnp.concatenate([v_ref[...], values[j // 2 * 2][here, :], values[j // 2 * 2 + 1][here, :]], axis=1)
            l_hi, l_lo = split(left)
            out_ref[...] = a_ref[...] - (dot(l_hi, hi) + (dot(l_lo, hi) + dot(l_hi, lo)))


def part_update(a, v, hi, lo, blocks, index, state):
    rows, cols = a.shape
    wide = v.shape[1]
    count = len(blocks)
    span, b = blocks[0][0].shape
    block = span // 2
    first = state is None
    placed = lambda i, index: (index[i], 0)
    fixed = lambda i, index: (0, 0)
    in_specs = [
        pl.BlockSpec((block, cols), placed),
        pl.BlockSpec((block, wide), placed),
        pl.BlockSpec((2 * wide, cols), fixed),
        pl.BlockSpec((2 * wide, cols), fixed),
    ] + [pl.BlockSpec((span, b), fixed)] * (2 * count)
    operands = [a, v, hi, lo] + [value for pair in blocks for value in pair]
    aliases = {}
    if not first:
        in_specs.append(pl.BlockSpec(memory_space=pl.ANY))
        operands.append(state)
        aliases = {len(operands): 0}
    return pl.pallas_call(
        functools.partial(part_update_kernel, count, first),
        grid_spec=pltpu.PrefetchScalarGridSpec(
            num_scalar_prefetch=1,
            grid=(2 * count,),
            in_specs=in_specs,
            out_specs=pl.BlockSpec((block, cols), placed),
        ),
        out_shape=jax.ShapeDtypeStruct((rows, cols), f32),
        input_output_aliases=aliases,
        compiler_params=pltpu.CompilerParams(vmem_limit_bytes=VMEM_LIMIT),
        name="part_update",
    )(index, *operands)


def all_sum(value):
    cols = lax.axis_size("col")
    core = lax.axis_index("col") % 2
    swap = [(c, c ^ 1) for c in range(cols)]
    rows = value.shape[0] // 2
    keep = lax.dynamic_slice_in_dim(value, core * rows, rows, 0)
    give = lax.dynamic_slice_in_dim(value, (1 - core) * rows, rows, 0)
    keep = keep + lax.ppermute(give, "col", swap)
    keep = keep + lax.ppermute(keep, "row", [(0, 1), (1, 0)])
    bit = 2
    while bit < cols:
        keep = keep + lax.ppermute(keep, "col", [(c, c ^ bit) for c in range(cols)])
        bit *= 2
    other = lax.ppermute(keep, "col", swap)
    return jnp.concatenate([jnp.where(core == 0, keep, other), jnp.where(core == 0, other, keep)], axis=0)


def body(matrix, vectors, tfactor):
    rows_here, cols_here = matrix.shape
    own, b = vectors.shape[1:]
    cols = lax.axis_size("col")
    row, col = lax.axis_index("row"), lax.axis_index("col")
    chips = cols // 2
    half = chips // 2
    chip, core = col // 2, col % 2
    both = ("row", "col")

    order = ring_order(chips)
    state = None

    def multiply(step, blocks):
        nonlocal state
        here = order[:1] if step == 0 else order[2 * step - 1 : 2 * step + 1]
        state = part_product(matrix, blocks, jnp.stack(here).astype(jnp.int32), state)
        return [state[2]]

    ring_work(chip_block(jnp.concatenate([vectors[0], vectors[1]], axis=1)), multiply)
    part, v_rows, _ = state

    keep = lax.dynamic_slice_in_dim(part, row * own, own, 1)
    give = lax.dynamic_slice_in_dim(part, (1 - row) * own, own, 1)
    across = [(0, 1), (1, 0)]
    sums = [keep[p * b : (p + 1) * b] + lax.ppermute(give[p * b : (p + 1) * b], "row", across) for p in range(2)]
    halves = [s.T for s in sums]

    def at(r, j, k):
        return r * cols + 2 * (j % chips) + k

    foreign = [(r, j, k) for r in range(2) for j in range((1 - r) * half, (2 - r) * half) for k in range(2)]
    direct = [(at(r, j, k), at(1 - r, j + half, k)) for r, j, k in foreign]
    along = [(at(r, j, k), at(r, j + half, k)) for r, j, k in foreign]
    over = [(at(r, j + half, k), at(1 - r, j + half, k)) for r, j, k in foreign]
    got1 = lax.ppermute(halves[0], both, direct)
    got2 = lax.ppermute(lax.ppermute(halves[1], both, along), both, over)
    home = chip // half == row
    z1 = jnp.where(home, halves[0], got1)
    z2 = jnp.where(home, halves[1], got2)

    def z_index(j, k):
        return 2 * (2 * (j % half) + k) + j // half

    small = all_sum(own_gram(z_index(chip, core).reshape(1).astype(jnp.int32), v_rows, z1, z2))

    owner = col // chips
    mine = lax.dynamic_slice_in_dim(v_rows, (col - owner * chips) * cols_here, cols_here, 0)
    mine, _ = lax.optimization_barrier((mine, z1))
    tile_pairs = [(r * cols + c, (1 - r) * cols + c) for r in range(2) for c in range(r * chips, (r + 1) * chips)]
    v_cols = jnp.where(owner == row, mine, lax.ppermute(mine, both, tile_pairs))
    sums = jnp.concatenate(sums, axis=0)
    others = lax.ppermute(sums, "row", across)
    zt = jnp.concatenate([jnp.where(row == 0, sums, others), jnp.where(row == 0, others, sums)], axis=1)

    z_blocks = list(zip(*ring_gather([z1, z2])))
    v_pair = jnp.stack([v_cols[:, :b], v_cols[:, b:]])
    hi, lo = factors(tfactor, small, small[b:, :b], zt, v_pair)
    index = jnp.stack([z_index(j, k) for j in order for k in range(2)]).astype(jnp.int32)
    return part_update(matrix, v_rows, hi, lo, z_blocks, index, None)


def solution(mesh):
    rows, cols = mesh.shape["row"], mesh.shape["col"]
    pairs = rows == 2 and cols >= 8 and cols & (cols - 1) == 0
    return jax.shard_map(
        body if pairs else general_body,
        mesh=mesh,
        in_specs=(P("row", "col"), P(None, ("row", "col"), None), P()),
        out_specs=P("row", "col"),
        check_vma=False,
    )
```
